32 devices in a mesh: lon: 4 (over y, x), lat: 8 (over z, core).
Axes of the slice: x: 2, y: 2, z: 4, core: 2. Of those that a mesh axis runs over, the one named last changes fastest.
Arguments:
- adjoint: float32 [4, 10, 512, 2048], P(None, None, 'lat', 'lon'), may hold values from -6 to 6
- trajectory: float32 [4, 10, 512, 2048], P(None, None, 'lat', 'lon'), may hold values from -6 to 6
- diffusivity: float32 [10, 512, 2048], P(None, 'lat', 'lon'), may hold values from 0.06 to 0.24
- land_mask: int32 [10, 512, 2048], P(None, 'lat', 'lon'), may hold values 0 or 1
- coriolis: float32 [512], P('lat'), may hold values from -0.3 to 0.3
- obs_values: float32 [4096, 128], P(('lon', 'lat')), may hold values from -6 to 6
- obs_weight: float32 [4096], P(('lon', 'lat')), may hold values from 0.5 to 4
- obs_owner: int32 [4096, 1], P(('lon', 'lat')), may hold values from 0 to 31; in each aligned block of 128 rows (0 to 127, 128 to 255, ...) at most 8 rows name the same one
- obs_offset: int32 [4096], P(('lon', 'lat')), may hold values from 0 to 10239
- fold_partner: int32 [2048], P('lon'), may hold values from 0 to 2047, as said below
Outputs:
- adjoint_out: float32 [4, 10, 512, 2048], P(None, None, 'lat', 'lon')
The draws below stay inside these ranges and needn't reach their ends.
Inputs may be any that keep to these rules, and one draw needn't show every extreme that they name: `obs_owner`: in the rows of one device no owner is named by more than 8 rows, a bound that some block reaches. fold_partner is the mirror of the tripolar fold: fold_partner[i] = (2047 - i + o) modulo 2048 for one even offset o.
All inputs are finite; a program needn't handle non-finite values. No bound on the sum of `land_mask` on one device may be relied on, other than what follows from the above.
Results may differ from the reference program's by a relative error of at most 0.000059.
Values sent between devices are 32-bit elements; how exact they have to be, the bound alone decides.
A program may use at most 320 MiB of HBM per device.

```python
import math
import jax
import jax.numpy as jnp
import numpy as np

FIELDS = 4
LEV = 10
NSUB = 3
SEG = 128
CAP = 8
CX = 512
CY = 64
NX = 2048
NY = 512
OBS_DEV = 128
OBS_ROWS = 4096
TILE_ROWS = 10240
N_LAT = 8
DEVICES = 32


def draw_fold_partner(key, part):
    offset_half = jax.random.randint(key, (), 0, NX // 2).astype(jnp.int32)
    longitudes = jnp.arange(NX, dtype=jnp.int32)
    partner = (NX - 1 - longitudes + 2 * offset_half) % NX
    return partner.astype(jnp.int32)


def plant(result, key, least, high):
    extent = result.shape
    index_at = [jax.random.randint(jax.random.fold_in(key, axis), (), 0, extent[axis]) for axis in range(len(extent))]
    result = result.at[tuple(index_at)].set(least)
    longest = extent.index(max(extent))
    index_at[longest] = (index_at[longest] + 1) % extent[longest]
    return result.at[tuple(index_at)].set(high)


def block_levels(key, dims, shards, low, largest):
    def one(axis_at, parts):
        heights = jax.random.uniform(jax.random.fold_in(jax.random.fold_in(key, 6), axis_at), (parts,), jnp.float32, low / len(shards), largest / len(shards))
        return jnp.repeat(jnp.exp(heights), dims[axis_at] // parts).reshape((-1,) + (1,) * (len(dims) - axis_at - 1))

    loudness = one(*shards[0])
    for cut in shards[1:]:
        loudness = loudness * one(*cut)
    return loudness


def routed_block(key, own, number, rows, number_of, top, bound, skew):
    sequence = jax.random.permutation(key, number_of)
    packed, common = portions_of(number_of, rows * top, bound, skew, True), portions_of(number_of, rows * top, bound, skew, False)
    places = jnp.arange(number_of)

    def named(sizes, offset_by):
        used = int((sizes > 0).sum())
        fixed = max(1, used // 4)
        shifted = fixed + (places - fixed + offset_by * (used - fixed)) % max(1, number_of - fixed)
        return jnp.zeros((number_of,), jnp.int32).at[sequence[jnp.where(places < fixed, places, shifted)]].set(jnp.asarray(sizes, jnp.int32))

    sizes = jnp.where(number % 4 == 0, named(packed, number // 4), named(common, number - number // 4 - 1))
    mixed = jax.random.permutation(jax.random.fold_in(own, 3), number_of)
    giver, receiver = mixed[0:number_of // 2 * 2:2], mixed[1:number_of // 2 * 2:2]
    slack = jnp.minimum(sizes[giver] - 1, bound - sizes[receiver]) // 2
    slack = jnp.where((giver == sequence[0]) | (receiver == sequence[0]) | (sizes[receiver] == 0), 0, jnp.maximum(slack, 0))
    shifted = jax.random.randint(jax.random.fold_in(own, 4), (number_of // 2,), 0, 1 << 20) % (slack + 1)
    sizes = sizes.at[giver].add(-shifted).at[receiver].add(shifted)
    members = jnp.searchsorted(jnp.cumsum(sizes), jnp.arange(rows * top), side="right").astype(jnp.int32)
    grid = members.reshape(top, rows).T
    grid = grid[jax.random.permutation(jax.random.fold_in(own, 1), rows)]
    offset_by = jax.random.randint(jax.random.fold_in(own, 2), (rows, 1), 0, top)
    return jnp.take_along_axis(grid, (jnp.arange(top)[None, :] + offset_by) % top, axis=1)


def portions_of(amount, total, limit, slope, full):
    weights = [(1 << 20) // math.isqrt(rank ** slope) + 1 for rank in range(1, amount + 1)]
    largest = limit if full else min(limit, max(-(-total // amount), total * weights[0] // sum(weights)))
    least = 1 if total - largest >= amount - 1 else 0
    counts, spare = [largest] + [least] * (amount - 1), total - largest - least * (amount - 1)
    while spare > 0:
        movable = [i for i in range(1, amount) if counts[i] < largest] or [i for i in range(1, amount) if counts[i] < limit]
        pool, left = sum([weights[i] for i in movable]), spare
        for i in movable:
            more = min(limit - counts[i], max(1, left * weights[i] // pool), spare)
            counts[i] = counts[i] + more
            spare = spare - more
    return np.array(counts)


def scatter_about(stream_key, extent, deviation, bound, cuts=(), kind=jnp.bfloat16):
    loudness = block_levels(stream_key, extent, cuts, -0.22, 0.18) if cuts else 1.0
    result = jax.random.normal(stream_key, extent, jnp.float32) * deviation * loudness
    return jnp.minimum(jnp.maximum(result, -bound), bound).astype(kind)


def setup_inputs(seed: int = 0) -> dict:
    seeds = jax.random.split(jax.random.key(seed), 11)
    adjoint = scatter_about(seeds[0], (FIELDS, LEV, NY, NX), 1.0, 6.0, ((2, 8), (3, 4)), jnp.float32)
    trajectory = scatter_about(seeds[1], (FIELDS, LEV, NY, NX), 1.0, 6.0, ((2, 8), (3, 4)), jnp.float32)
    diffusivity = jnp.clip(jnp.exp(math.log(0.24) - 1.3862944 * jax.random.uniform(seeds[2], (LEV, NY, NX), jnp.float32) ** block_levels(seeds[2], (LEV, NY, NX), ((1, 8), (2, 4)), -0.2, 0.2)), 0.06, 0.24)
    land_mask = plant((jax.random.randint(seeds[3], (LEV, NY, NX), 0, 4) < 3).astype(jnp.int32), jax.random.fold_in(seeds[3], 1), 0, 1)
    coriolis = jnp.clip(jax.random.uniform(seeds[4], (NY,), jnp.float32, -0.3, 0.3) * block_levels(seeds[4], (NY,), ((0, 8),), -0.4, 0.0), -0.3, 0.3)
    obs_values = scatter_about(seeds[5], (OBS_ROWS, SEG), 1.0, 6.0, ((0, 32),), jnp.float32)
    obs_weight = jnp.clip(jnp.exp(math.log(4.0) - 2.0794415 * jax.random.uniform(seeds[6], (OBS_ROWS,), jnp.float32) ** block_levels(seeds[6], (OBS_ROWS,), ((0, 32),), -0.2, 0.2)), 0.5, 4.0)
    obs_owner_keys = jax.random.split(jax.random.fold_in(seeds[7], 1), OBS_ROWS // OBS_DEV)
    obs_owner_turns = jax.random.permutation(jax.random.fold_in(seeds[7], 3), OBS_ROWS // OBS_DEV)
    obs_owner = jax.vmap(lambda own, number: routed_block(jax.random.fold_in(seeds[7], 2), own, number, OBS_DEV, DEVICES, 1, CAP, 2))(obs_owner_keys, obs_owner_turns).reshape((OBS_ROWS, 1))
    obs_offset = plant(jax.random.randint(seeds[8], (OBS_ROWS,), 0, TILE_ROWS), jax.random.fold_in(seeds[8], 1), 0, TILE_ROWS - 1).astype(jnp.int32)
    fold_partner = draw_fold_partner(jax.random.fold_in(seeds[10], 71), 0)
    return {"adjoint": adjoint, "trajectory": trajectory, "diffusivity": diffusivity, "land_mask": land_mask, "coriolis": coriolis, "obs_values": obs_values, "obs_weight": obs_weight, "obs_owner": obs_owner, "obs_offset": obs_offset, "fold_partner": fold_partner}


def reference(adjoint, trajectory, diffusivity, land_mask, coriolis, obs_values, obs_weight, obs_owner, obs_offset, fold_partner):
    wet_cells = land_mask.astype(jnp.float32)
    field_sign = jnp.array([1.0, 1.0, -1.0, -1.0], jnp.float32).reshape(4, 1, 1, 1)
    work_state = adjoint * wet_cells[None]
    for sweep_index in range(NSUB):
        ghost_rows = field_sign * jnp.take(work_state[:, :, NY - 1:NY, :], fold_partner, axis=3)
        northern = jnp.concatenate([work_state[:, :, 1:, :], ghost_rows], axis=2)
        southern = jnp.concatenate([jnp.zeros_like(work_state[:, :, :1, :]), work_state[:, :, :-1, :]], axis=2)
        eastern = jnp.roll(work_state, -1, axis=3)
        western = jnp.roll(work_state, 1, axis=3)
        laplace = eastern + western + northern + southern - 4.0 * work_state
        work_state = work_state + diffusivity[None] * laplace
    rotation = coriolis[:, None]
    adjoint_u = work_state[2] - rotation * work_state[3]
    adjoint_v = work_state[3] + rotation * work_state[2]
    mixed = jnp.stack([work_state[0], work_state[1], adjoint_u, adjoint_v])
    segments = CX // SEG
    owner_index = obs_owner[:, 0]
    lon_tile = owner_index // N_LAT
    lat_band = owner_index % N_LAT
    seg_local = obs_offset % segments
    rest_index = obs_offset // segments
    row_local = rest_index % CY
    layer_index = rest_index // CY
    glob_row = (lat_band * CY + row_local).astype(jnp.int32)
    glob_seg = (lon_tile * segments + seg_local).astype(jnp.int32)
    traj_view = trajectory.reshape(FIELDS * LEV, NY, NX // SEG, SEG)
    misfit = obs_weight[:, None] * (traj_view[layer_index, glob_row, glob_seg] - obs_values)
    forcing = jnp.zeros_like(traj_view).at[layer_index, glob_row, glob_seg].add(misfit)
    forcing = forcing.reshape(FIELDS, LEV, NY, NX)
    return wet_cells[None] * (mixed + forcing)
```

```python
import functools

import jax
import jax.numpy as jnp
from jax import lax
from jax.experimental import pallas as pl
from jax.experimental.pallas import tpu as pltpu
from jax.sharding import PartitionSpec as P

NSUB = 3
CAP = 8
LANES = 128
MESH = pl.DeviceIdType.MESH
VMEM = pltpu.VMEM
F32 = jnp.float32


def dot(left, right, dims, precision=lax.Precision.HIGHEST):
    return lax.dot_general(
        left, right, (dims, ((), ())), precision=precision, preferred_element_type=F32
    )


def pack_kernel(
    n, levels,
    adj_top, adj_bot, adj_w, adj_e, wet_top, wet_bot, wet_w, wet_e,
    dif_top, dif_bot, dif_w, dif_e, owner, weight, offset, values,
    row_top, row_bot, col_w, col_e, obs,
):
    layers = adj_top.shape[0]
    for out in (row_top, row_bot):
        out[...] = jnp.zeros_like(out)

    def state_level(layer, carry):
        k = lax.rem(layer, levels)
        top = adj_top[layer] * wet_top[k].astype(F32)
        bot = adj_bot[layer] * wet_bot[k].astype(F32)
        for r in range(NSUB):
            row_top[r, pl.ds(layer, 1), :] = top[8 - NSUB + r : 8 - NSUB + r + 1]
            row_bot[r, pl.ds(layer, 1), :] = bot[r : r + 1]
        return columns(
            layer, adj_w[layer] * wet_w[k].astype(F32), adj_e[layer] * wet_e[k].astype(F32), carry
        )

    def columns(place, west, east, carry):
        lane = lax.broadcasted_iota(jnp.int32, west.shape, 1)
        first = NSUB * place
        here = (lane >= first) & (lane < first + NSUB)
        west = pltpu.roll(west, first, 1)
        east = pltpu.roll(east, lax.rem(first + NSUB, LANES), 1)
        return jnp.where(here, west, carry[0]), jnp.where(here, east, carry[1])

    def dif_level(k, carry):
        top, bot = dif_top[k], dif_bot[k]
        for r in range(NSUB):
            row_top[r, pl.ds(layers + k, 1), :] = top[8 - NSUB + r : 8 - NSUB + r + 1]
            row_bot[r, pl.ds(layers + k, 1), :] = bot[r : r + 1]
        return columns(k, dif_w[k], dif_e[k], carry)

    zero = jnp.zeros(adj_w.shape[1:], F32)
    west, east = lax.fori_loop(0, layers, state_level, (zero, zero))
    col_w[:, :LANES], col_e[:, :LANES] = west, east
    west, east = lax.fori_loop(0, levels, dif_level, (zero, zero))
    col_w[:, LANES:], col_e[:, LANES:] = west, east

    rows = values.shape[0]
    own = owner[...]
    one_hot = (lax.broadcasted_iota(jnp.int32, (n, rows), 0) == own).astype(F32)
    earlier_than = (
        lax.broadcasted_iota(jnp.int32, (rows, rows), 0)
        < lax.broadcasted_iota(jnp.int32, (rows, rows), 1)
    ).astype(F32)
    earlier = dot(one_hot, earlier_than, ((1,), (0,)), lax.Precision.DEFAULT)
    slot = jnp.sum(earlier * one_hot, axis=0, keepdims=True).astype(jnp.int32)
    dest = own * CAP + slot
    hit = lax.broadcasted_iota(jnp.int32, (n * CAP, rows), 0) == dest
    sent = dot(hit.astype(F32), values[...], ((1,), (0,)))
    w = jnp.sum(jnp.where(hit, weight[...], 0.0), axis=1, keepdims=True)
    o = jnp.sum(jnp.where(hit, offset[...].astype(F32), 0.0), axis=1, keepdims=True)
    lane = lax.broadcasted_iota(jnp.int32, (n * CAP, LANES), 1)
    meta = jnp.where(lane == 0, w, o)
    obs[:, :CAP, :] = sent.reshape(n, CAP, LANES)
    obs[:, CAP:, :] = meta.reshape(n, CAP, LANES)


def exchange_kernel(
    n_lon, n_lat,
    row_top, row_bot, col_w, col_e, obs,
    north, south, west, east, corner_nw, corner_ne, corner_sw, corner_se, fold, got,
    send_sem, recv_sem, fold_send, fold_recv, obs_send, obs_recv, local_sem,
):
    n = n_lon * n_lat
    lon, lat = lax.axis_index("lon"), lax.axis_index("lat")
    me = lon * n_lat + lat
    right, left = lax.rem(lon + 1, n_lon), lax.rem(lon + n_lon - 1, n_lon)
    low, high = lat == 0, lat == n_lat - 1
    up, down = lax.rem(lat + 1, n_lat), lax.rem(lat + n_lat - 1, n_lat)

    barrier = pltpu.get_barrier_semaphore()

    @pl.loop(1, n)
    def _(step):
        peer = lax.rem(me + step, n)
        pl.semaphore_signal(
            barrier, inc=1, device_id=(peer // n_lat, lax.rem(peer, n_lat)), device_id_type=MESH
        )

    pl.semaphore_wait(barrier, n - 1)

    def remote(src, dst, sems, rsems, i, target):
        return pltpu.make_async_remote_copy(
            src_ref=src, dst_ref=dst, send_sem=sems.at[i], recv_sem=rsems.at[i],
            device_id=target, device_id_type=MESH,
        )

    halo = functools.partial(
        lambda i, src, dst, target: remote(src, dst, send_sem, recv_sem, i, target)
    )
    last = col_w.shape[0] - 8
    lifted = [
        halo(0, row_top, south, (lon, up)),
        halo(1, col_e.at[pl.ds(last, 8)], corner_sw, (right, up)),
        halo(2, col_w.at[pl.ds(last, 8)], corner_se, (left, up)),
    ]
    lowered = [
        halo(3, row_bot, north, (lon, down)),
        halo(4, col_e.at[pl.ds(0, 8)], corner_nw, (right, down)),
        halo(5, col_w.at[pl.ds(0, 8)], corner_ne, (left, down)),
    ]
    level = [halo(6, col_e, west, (right, lat)), halo(7, col_w, east, (left, lat))]

    def fold_copy(step, slot):
        peer = lax.rem(lon + step, n_lon)
        return remote(row_top, fold.at[slot], fold_send, fold_recv, step, (peer, lat))

    def obs_copy(step, slot):
        peer = lax.rem(me + step, n)
        return remote(
            obs.at[peer], got.at[slot], obs_send, obs_recv, step,
            (peer // n_lat, lax.rem(peer, n_lat)),
        )

    own_fold = pltpu.make_async_copy(row_top, fold.at[lon], local_sem.at[0])
    own_obs = pltpu.make_async_copy(obs.at[me], got.at[me], local_sem.at[1])

    @pl.when(high)
    def _():
        for step in range(1, n_lon):
            fold_copy(step, lon).start()
        own_fold.start()

    @pl.when(jnp.logical_not(high))
    def _():
        for copy in lifted:
            copy.start()

    @pl.when(jnp.logical_not(low))
    def _():
        for copy in lowered:
            copy.start()

    for copy in level:
        copy.start()

    @pl.loop(1, n)
    def _(step):
        obs_copy(step, me).start()

    own_obs.start()

    @pl.when(high)
    def _():
        for step in range(1, n_lon):
            fold_copy(step, lax.rem(lon + n_lon - step, n_lon)).wait_recv()
            fold_copy(step, lon).wait_send()
        own_fold.wait()

    @pl.when(jnp.logical_not(high))
    def _():
        for copy in lifted:
            copy.wait_send()
        for copy in lowered:
            copy.wait_recv()

    @pl.when(jnp.logical_not(low))
    def _():
        for copy in lowered:
            copy.wait_send()
        for copy in lifted:
            copy.wait_recv()

    for copy in level:
        copy.wait()

    @pl.loop(1, n)
    def _(step):
        obs_copy(step, lax.rem(me + n - step, n)).wait_recv()
        obs_copy(step, me).wait_send()

    own_obs.wait()


def main_kernel(
    n, n_lon, n_lat, layers,
    got_offset, got_weight, partner,
    adj, dif, wet_ref, coriolis, traj, got,
    north, south, west, east, corner_nw, corner_ne, corner_sw, corner_se, fold,
    out, forcing, rim, ext,
):
    k = pl.program_id(0)
    fields, _, cy, cx = adj.shape
    levels = layers // fields
    lat = lax.axis_index("lat")
    low, high = lat == 0, lat == n_lat - 1
    wide = cx + LANES
    segs = cx // LANES
    sub8 = lax.broadcasted_iota(jnp.int32, (8, LANES), 0)

    @pl.when(k == 0)
    def _():
        forcing[...] = jnp.zeros_like(forcing)
        ext[...] = jnp.zeros_like(ext)

        @pl.loop(0, n)
        def _(block):
            for s in range(CAP):
                place = got_offset[block * CAP + s]
                lanes = pl.ds(pl.multiple_of(lax.rem(place, segs) * LANES, LANES), LANES)
                rest = place // segs
                y, layer = lax.rem(rest, cy), rest // cy
                tile = pl.ds(pl.multiple_of(y // 8 * 8, 8), 8)
                misfit = got_weight[block * CAP + s] * (
                    traj[layer, tile, lanes] - got[block, s : s + 1, :]
                )
                forcing[layer, tile, lanes] = forcing[layer, tile, lanes] + jnp.where(
                    sub8 == lax.rem(y, 8), misfit, 0.0
                )

        @pl.when(jnp.logical_not(high))
        def _():
            rim[:, :, :cx] = north[...]

        @pl.when(high)
        def _():
            nx = n_lon * cx
            lane = lax.broadcasted_iota(jnp.int32, (cx, wide), 1)
            lane = jnp.where(lane < cx + LANES // 2, lane, lane - wide)
            column = partner[0] - lane
            column = jnp.where(column < 0, column + nx, column)
            column = jnp.where(column >= nx, column - nx, column)
            within = lax.broadcasted_iota(jnp.int32, (cx, wide), 0)
            for r in range(NSUB):
                total = jnp.zeros((fold.shape[2], wide), F32)
                for t in range(n_lon):
                    pick = (within + t * cx == column).astype(F32).astype(jnp.bfloat16)
                    left = fold[t, NSUB - 1 - r]
                    for part in range(3):
                        piece = left.astype(jnp.bfloat16)
                        left = left - piece.astype(F32)
                        total = total + dot(piece, pick, ((1,), (0,)), None)
                rim[r] = total

    lane = lax.broadcasted_iota(jnp.int32, (cy, LANES), 1)
    lane8 = lax.broadcasted_iota(jnp.int32, (8, LANES), 1)

    def surround(place, row, side, sign):
        cols = pl.ds(side * LANES, LANES)
        shift_e = lax.rem(LANES - NSUB * place, LANES)
        shift_w = lax.rem(2 * LANES - NSUB - NSUB * place, LANES)
        ext[:cy, cx:] = jnp.where(
            lane < LANES // 2,
            pltpu.roll(east[:, cols], shift_e, 1),
            pltpu.roll(west[:, cols], shift_w, 1),
        )

        def corner(e_ref, w_ref, absent):
            both = jnp.where(
                lane8 < LANES // 2,
                pltpu.roll(e_ref[:, cols], shift_e, 1),
                pltpu.roll(w_ref[:, cols], shift_w, 1),
            )
            return jnp.where(absent, 0.0, both)

        ext[cy:, cx:] = jnp.where(
            sub8 < 4,
            corner(corner_ne, corner_nw, high),
            corner(corner_se, corner_sw, low),
        )
        for r in range(NSUB):
            ext[cy + r : cy + r + 1, :cx] = sign * rim[r, pl.ds(row, 1), :][:, :cx]
            line = south[r, pl.ds(row, 1), :]
            at = cy + 8 - NSUB + r
            ext[at : at + 1, :cx] = jnp.where(low, 0.0, line)

        @pl.when(high)
        def _():
            for r in range(NSUB):
                ext[cy + r : cy + r + 1, cx:] = sign * rim[r, pl.ds(row, 1), :][:, cx:]

    ext[:cy, :cx] = dif[0]
    surround(k, layers + k, 1, 1.0)
    coeffs = ext[...]
    wet = wet_ref[0].astype(F32)
    mixed = []
    for f in range(fields):
        ext[:cy, :cx] = adj[f, 0] * wet
        layer = f * levels + k
        surround(layer, layer, 0, jnp.where(high, 1.0 if f < 2 else -1.0, 1.0))
        work = ext[...]
        for _ in range(NSUB):
            near = (
                pltpu.roll(work, wide - 1, 1)
                + pltpu.roll(work, 1, 1)
                + pltpu.roll(work, cy + 7, 0)
                + pltpu.roll(work, 1, 0)
            )
            work = work + coeffs * (near - 4.0 * work)
        mixed.append(work[:cy, :cx])
    line = coriolis[...]
    square = lax.broadcasted_iota(jnp.int32, (cy, cy), 0) == lax.broadcasted_iota(
        jnp.int32, (cy, cy), 1
    )
    turn = jnp.sum(jnp.where(square, line, 0.0), axis=1, keepdims=True)
    u, v = mixed[2] - turn * mixed[3], mixed[3] + turn * mixed[2]
    for f, m in enumerate((mixed[0], mixed[1], u, v)):
        out[f, 0] = wet * (m + forcing[f * levels + k])


def per_device(
    n_lon, n_lat,
    adjoint, trajectory, diffusivity, land_mask, coriolis,
    obs_values, obs_weight, obs_owner, obs_offset, fold_partner,
):
    n = n_lon * n_lat
    fields, levels, cy, cx = adjoint.shape
    layers = fields * levels
    rows = obs_values.shape[0]
    adj3 = adjoint.reshape(layers, cy, cx)
    traj3 = trajectory.reshape(layers, cy, cx)

    def edges(depth):
        top = pl.BlockSpec((depth, 8, cx), lambda i: (0, cy // 8 - 1, 0))
        bot = pl.BlockSpec((depth, 8, cx), lambda i: (0, 0, 0))
        west = pl.BlockSpec((depth, cy, LANES), lambda i: (0, 0, 0))
        east = pl.BlockSpec((depth, cy, LANES), lambda i: (0, 0, cx // LANES - 1))
        return [top, bot, west, east]

    def whole(shape):
        return pl.BlockSpec(shape, lambda i: (0,) * len(shape))

    def f32(*shape):
        return jax.ShapeDtypeStruct(shape, F32)

    packed = -(-(layers + levels) // 8) * 8
    row_shape, col_shape, obs_shape = (NSUB, packed, cx), (cy, 2 * LANES), (n, 2 * CAP, LANES)
    shapes = [row_shape, row_shape, col_shape, col_shape, obs_shape]
    packs = pl.pallas_call(
        functools.partial(pack_kernel, n, levels),
        grid=(1,),
        out_shape=[f32(*s) for s in shapes],
        in_specs=edges(layers) + edges(levels) + edges(levels)
        + [whole((1, rows))] * 3 + [whole((rows, LANES))],
        out_specs=[whole(s) for s in shapes],
        compiler_params=pltpu.CompilerParams(vmem_limit_bytes=48 << 20),
        name="pack",
    )(
        *[adj3] * 4, *[land_mask] * 4, *[diffusivity] * 4,
        obs_owner.reshape(1, rows), obs_weight.reshape(1, rows), obs_offset.reshape(1, rows),
        obs_values,
    )

    corner = (8, 2 * LANES)
    came = [row_shape, row_shape, col_shape, col_shape, corner, corner, corner, corner]
    fold_shape = (n_lon,) + row_shape
    *halos, fold, got = pl.pallas_call(
        functools.partial(exchange_kernel, n_lon, n_lat),
        out_shape=[f32(*s) for s in came + [fold_shape, obs_shape]],
        in_specs=[pl.BlockSpec(memory_space=pl.ANY)] * 5,
        out_specs=[pl.BlockSpec(memory_space=pl.ANY)] * 10,
        scratch_shapes=[
            pltpu.SemaphoreType.DMA((8,)), pltpu.SemaphoreType.DMA((8,)),
            pltpu.SemaphoreType.DMA((n_lon,)), pltpu.SemaphoreType.DMA((n_lon,)),
            pltpu.SemaphoreType.DMA((n,)), pltpu.SemaphoreType.DMA((n,)),
            pltpu.SemaphoreType.DMA((2,)),
        ],
        compiler_params=pltpu.CompilerParams(collective_id=0, has_side_effects=True),
        name="exchange",
    )(*packs)

    got_weight = got[:, CAP:, 0].reshape(n * CAP)
    got_offset = got[:, CAP:, 1].reshape(n * CAP).astype(jnp.int32)
    smem = pl.BlockSpec(memory_space=pltpu.SMEM)
    level3 = pl.BlockSpec((1, cy, cx), lambda i: (i, 0, 0))
    level4 = pl.BlockSpec((fields, 1, cy, cx), lambda i: (0, i, 0, 0))
    return pl.pallas_call(
        functools.partial(main_kernel, n, n_lon, n_lat, layers),
        grid=(levels,),
        out_shape=f32(*adjoint.shape),
        in_specs=[smem, smem, smem, level4, level3, level3, whole((1, cy)),
                  whole((layers, cy, cx)), whole(obs_shape)]
        + [whole(s) for s in came] + [whole(fold_shape)],
        out_specs=level4,
        scratch_shapes=[
            VMEM((layers, cy, cx), F32),
            VMEM((NSUB, packed, cx + LANES), F32),
            VMEM((cy + 8, cx + LANES), F32),
        ],
        compiler_params=pltpu.CompilerParams(vmem_limit_bytes=56 << 20),
        name="mix",
    )(
        got_offset, got_weight, fold_partner, adjoint, diffusivity, land_mask,
        coriolis.reshape(1, cy), traj3, got, *halos, fold,
    )


def solution(mesh):
    return jax.shard_map(
        functools.partial(per_device, mesh.shape["lon"], mesh.shape["lat"]),
        mesh=mesh,
        in_specs=(
            P(None, None, "lat", "lon"),
            P(None, None, "lat", "lon"),
            P(None, "lat", "lon"),
            P(None, "lat", "lon"),
            P("lat"),
            P(("lon", "lat"), None),
            P(("lon", "lat")),
            P(("lon", "lat"), None),
            P(("lon", "lat")),
            P("lon"),
        ),
        out_specs=P(None, None, "lat", "lon"),
        check_vma=False,
    )
```

```python
import functools

import jax
import jax.numpy as jnp
from jax import lax
from jax.experimental import pallas as pl
from jax.experimental.pallas import tpu as pltpu
from jax.sharding import PartitionSpec as P

NSUB = 3
CAP = 8
LANES = 128
MESH = pl.DeviceIdType.MESH
VMEM = pltpu.VMEM
F32 = jnp.float32


def dot(left, right, dims, precision=lax.Precision.HIGHEST):
    return lax.dot_general(
        left, right, (dims, ((), ())), precision=precision, preferred_element_type=F32
    )


def pack_kernel(
    n, levels,
    adj_top, adj_bot, adj_w, adj_e, wet_top, wet_bot, wet_w, wet_e,
    dif_top, dif_bot, dif_w, dif_e, owner, weight, offset, values,
    row_top, row_bot, col_w, col_e, obs,
):
    layers = adj_top.shape[0]
    for out in (row_top, row_bot):
        out[...] = jnp.zeros_like(out)

    def state_level(layer, carry):
        k = lax.rem(layer, levels)
        top = adj_top[layer] * wet_top[k].astype(F32)
        bot = adj_bot[layer] * wet_bot[k].astype(F32)
        for r in range(NSUB):
            row_top[r, pl.ds(layer, 1), :] = top[8 - NSUB + r : 8 - NSUB + r + 1]
            row_bot[r, pl.ds(layer, 1), :] = bot[r : r + 1]
        return columns(
            layer, adj_w[layer] * wet_w[k].astype(F32), adj_e[layer] * wet_e[k].astype(F32), carry
        )

    def columns(place, west, east, carry):
        lane = lax.broadcasted_iota(jnp.int32, west.shape, 1)
        first = NSUB * place
        here = (lane >= first) & (lane < first + NSUB)
        west = pltpu.roll(west, first, 1)
        east = pltpu.roll(east, lax.rem(first + NSUB, LANES), 1)
        return jnp.where(here, west, carry[0]), jnp.where(here, east, carry[1])

    def dif_level(k, carry):
        top, bot = dif_top[k], dif_bot[k]
        for r in range(NSUB):
            row_top[r, pl.ds(layers + k, 1), :] = top[8 - NSUB + r : 8 - NSUB + r + 1]
            row_bot[r, pl.ds(layers + k, 1), :] = bot[r : r + 1]
        return columns(k, dif_w[k], dif_e[k], carry)

    zero = jnp.zeros(adj_w.shape[1:], F32)
    west, east = lax.fori_loop(0, layers, state_level, (zero, zero))
    col_w[:, :LANES], col_e[:, :LANES] = west, east
    west, east = lax.fori_loop(0, levels, dif_level, (zero, zero))
    col_w[:, LANES:], col_e[:, LANES:] = west, east

    rows = values.shape[0]
    own = owner[...]
    one_hot = (lax.broadcasted_iota(jnp.int32, (n, rows), 0) == own).astype(F32)
    earlier_than = (
        lax.broadcasted_iota(jnp.int32, (rows, rows), 0)
        < lax.broadcasted_iota(jnp.int32, (rows, rows), 1)
    ).astype(F32)
    earlier = dot(one_hot, earlier_than, ((1,), (0,)), lax.Precision.DEFAULT)
    slot = jnp.sum(earlier * one_hot, axis=0, keepdims=True).astype(jnp.int32)
    dest = own * CAP + slot
    hit = lax.broadcasted_iota(jnp.int32, (n * CAP, rows), 0) == dest
    sent = dot(hit.astype(F32), values[...], ((1,), (0,)))
    w = jnp.sum(jnp.where(hit, weight[...], 0.0), axis=1, keepdims=True)
    o = jnp.sum(jnp.where(hit, offset[...].astype(F32), 0.0), axis=1, keepdims=True)
    lane = lax.broadcasted_iota(jnp.int32, (n * CAP, LANES), 1)
    meta = jnp.where(lane == 0, w, o)
    obs[:, :CAP, :] = sent.reshape(n, CAP, LANES)
    obs[:, CAP:, :] = meta.reshape(n, CAP, LANES)


def exchange_kernel(
    n_lon, n_lat,
    row_top, row_bot, col_w, col_e, obs,
    north, south, west, east, corner_nw, corner_ne, corner_sw, corner_se, fold, got,
    send_sem, recv_sem, fold_send, fold_recv, obs_send, obs_recv, local_sem,
):
    n = n_lon * n_lat
    lon, lat = lax.axis_index("lon"), lax.axis_index("lat")
    me = lon * n_lat + lat
    right, left = lax.rem(lon + 1, n_lon), lax.rem(lon + n_lon - 1, n_lon)
    low, high = lat == 0, lat == n_lat - 1
    up, down = lax.rem(lat + 1, n_lat), lax.rem(lat + n_lat - 1, n_lat)

    barrier = pltpu.get_barrier_semaphore()

    @pl.loop(1, n)
    def _(step):
        peer = lax.rem(me + step, n)
        pl.semaphore_signal(
            barrier, inc=1, device_id=(peer // n_lat, lax.rem(peer, n_lat)), device_id_type=MESH
        )

    pl.semaphore_wait(barrier, n - 1)

    def remote(src, dst, sems, rsems, i, target):
        return pltpu.make_async_remote_copy(
            src_ref=src, dst_ref=dst, send_sem=sems.at[i], recv_sem=rsems.at[i],
            device_id=target, device_id_type=MESH,
        )

    halo = functools.partial(
        lambda i, src, dst, target: remote(src, dst, send_sem, recv_sem, i, target)
    )
    last = col_w.shape[0] - 8
    lifted = [
        halo(0, row_top, south, (lon, up)),
        halo(1, col_e.at[pl.ds(last, 8)], corner_sw, (right, up)),
        halo(2, col_w.at[pl.ds(last, 8)], corner_se, (left, up)),
    ]
    lowered = [
        halo(3, row_bot, north, (lon, down)),
        halo(4, col_e.at[pl.ds(0, 8)], corner_nw, (right, down)),
        halo(5, col_w.at[pl.ds(0, 8)], corner_ne, (left, down)),
    ]
    level = [halo(6, col_e, west, (right, lat)), halo(7, col_w, east, (left, lat))]

    def fold_copy(step, slot):
        peer = lax.rem(lon + step, n_lon)
        return remote(row_top, fold.at[slot], fold_send, fold_recv, step, (peer, lat))

    def obs_copy(step, slot):
        peer = lax.rem(me + step, n)
        return remote(
            obs.at[peer], got.at[slot], obs_send, obs_recv, step,
            (peer // n_lat, lax.rem(peer, n_lat)),
        )

    own_fold = pltpu.make_async_copy(row_top, fold.at[lon], local_sem.at[0])
    own_obs = pltpu.make_async_copy(obs.at[me], got.at[me], local_sem.at[1])

    @pl.when(high)
    def _():
        for step in range(1, n_lon):
            fold_copy(step, lon).start()
        own_fold.start()

    @pl.when(jnp.logical_not(high))
    def _():
        for copy in lifted:
            copy.start()

    @pl.when(jnp.logical_not(low))
    def _():
        for copy in lowered:
            copy.start()

    for copy in level:
        copy.start()

    @pl.loop(1, n)
    def _(step):
        obs_copy(step, me).start()

    own_obs.start()

    @pl.when(high)
    def _():
        for step in range(1, n_lon):
            fold_copy(step, lax.rem(lon + n_lon - step, n_lon)).wait_recv()
            fold_copy(step, lon).wait_send()
        own_fold.wait()

    @pl.when(jnp.logical_not(high))
    def _():
        for copy in lifted:
            copy.wait_send()
        for copy in lowered:
            copy.wait_recv()

    @pl.when(jnp.logical_not(low))
    def _():
        for copy in lowered:
            copy.wait_send()
        for copy in lifted:
            copy.wait_recv()

    for copy in level:
        copy.wait()

    @pl.loop(1, n)
    def _(step):
        obs_copy(step, lax.rem(me + n - step, n)).wait_recv()
        obs_copy(step, me).wait_send()

    own_obs.wait()


def main_kernel(
    n, n_lon, n_lat, layers,
    meta, partner,
    adj, dif, wet_ref, coriolis, traj, got,
    north, south, west, east, corner_nw, corner_ne, corner_sw, corner_se, fold,
    out, forcing, rim, ext,
):
    k = pl.program_id(0)
    fields, _, cy, cx = adj.shape
    levels = layers // fields
    lat = lax.axis_index("lat")
    low, high = lat == 0, lat == n_lat - 1
    wide = cx + LANES
    segs = cx // LANES
    sub8 = lax.broadcasted_iota(jnp.int32, (8, LANES), 0)

    @pl.when(k == 0)
    def _():
        forcing[...] = jnp.zeros_like(forcing)
        ext[...] = jnp.zeros_like(ext)

        @pl.loop(0, n)
        def _(block):
            for s in range(CAP):
                place = meta[(block * CAP + s) * 2 + 1].astype(jnp.int32)
                lanes = pl.ds(pl.multiple_of(lax.rem(place, segs) * LANES, LANES), LANES)
                rest = place // segs
                y, layer = lax.rem(rest, cy), rest // cy
                tile = pl.ds(pl.multiple_of(y // 8 * 8, 8), 8)
                misfit = meta[(block * CAP + s) * 2] * (
                    traj[layer, tile, lanes] - got[block, s : s + 1, :]
                )
                forcing[layer, tile, lanes] = forcing[layer, tile, lanes] + jnp.where(
                    sub8 == lax.rem(y, 8), misfit, 0.0
                )

        @pl.when(jnp.logical_not(high))
        def _():
            rim[:, :, :cx] = north[...]

        @pl.when(high)
        def _():
            nx = n_lon * cx
            lane = lax.broadcasted_iota(jnp.int32, (cx, wide), 1)
            lane = jnp.where(lane < cx + LANES // 2, lane, lane - wide)
            column = partner[0] - lane
            column = jnp.where(column < 0, column + nx, column)
            column = jnp.where(column >= nx, column - nx, column)
            within = lax.broadcasted_iota(jnp.int32, (cx, wide), 0)
            for r in range(NSUB):
                total = jnp.zeros((fold.shape[2], wide), F32)
                for t in range(n_lon):
                    pick = (within + t * cx == column).astype(F32).astype(jnp.bfloat16)
                    left = fold[t, NSUB - 1 - r]
                    for part in range(3):
                        piece = left.astype(jnp.bfloat16)
                        left = left - piece.astype(F32)
                        total = total + dot(piece, pick, ((1,), (0,)), None)
                rim[r] = total

    lane = lax.broadcasted_iota(jnp.int32, (cy, LANES), 1)
    lane8 = lax.broadcasted_iota(jnp.int32, (8, LANES), 1)

    def surround(place, row, side, sign):
        cols = pl.ds(side * LANES, LANES)
        shift_e = lax.rem(LANES - NSUB * place, LANES)
        shift_w = lax.rem(2 * LANES - NSUB - NSUB * place, LANES)
        ext[:cy, cx:] = jnp.where(
            lane < LANES // 2,
            pltpu.roll(east[:, cols], shift_e, 1),
            pltpu.roll(west[:, cols], shift_w, 1),
        )

        def corner(e_ref, w_ref, absent):
            both = jnp.where(
                lane8 < LANES // 2,
                pltpu.roll(e_ref[:, cols], shift_e, 1),
                pltpu.roll(w_ref[:, cols], shift_w, 1),
            )
            return jnp.where(absent, 0.0, both)

        ext[cy:, cx:] = jnp.where(
            sub8 < 4,
            corner(corner_ne, corner_nw, high),
            corner(corner_se, corner_sw, low),
        )
        for r in range(NSUB):
            ext[cy + r : cy + r + 1, :cx] = sign * rim[r, pl.ds(row, 1), :][:, :cx]
            line = south[r, pl.ds(row, 1), :]
            at = cy + 8 - NSUB + r
            ext[at : at + 1, :cx] = jnp.where(low, 0.0, line)

        @pl.when(high)
        def _():
            for r in range(NSUB):
                ext[cy + r : cy + r + 1, cx:] = sign * rim[r, pl.ds(row, 1), :][:, cx:]

    ext[:cy, :cx] = dif[0]
    surround(k, layers + k, 1, 1.0)
    coeffs = ext[...]
    wet = wet_ref[0].astype(F32)
    mixed = []
    for f in range(fields):
        ext[:cy, :cx] = adj[f, 0] * wet
        layer = f * levels + k
        surround(layer, layer, 0, jnp.where(high, 1.0 if f < 2 else -1.0, 1.0))
        work = ext[...]
        for _ in range(NSUB):
            near = (
                pltpu.roll(work, wide - 1, 1)
                + pltpu.roll(work, 1, 1)
                + pltpu.roll(work, cy + 7, 0)
                + pltpu.roll(work, 1, 0)
            )
            work = work + coeffs * (near - 4.0 * work)
        mixed.append(work[:cy, :cx])
    line = coriolis[...]
    square = lax.broadcasted_iota(jnp.int32, (cy, cy), 0) == lax.broadcasted_iota(
        jnp.int32, (cy, cy), 1
    )
    turn = jnp.sum(jnp.where(square, line, 0.0), axis=1, keepdims=True)
    u, v = mixed[2] - turn * mixed[3], mixed[3] + turn * mixed[2]
    for f, m in enumerate((mixed[0], mixed[1], u, v)):
        out[f, 0] = wet * (m + forcing[f * levels + k])


def per_device(
    n_lon, n_lat,
    adjoint, trajectory, diffusivity, land_mask, coriolis,
    obs_values, obs_weight, obs_owner, obs_offset, fold_partner,
):
    n = n_lon * n_lat
    fields, levels, cy, cx = adjoint.shape
    layers = fields * levels
    rows = obs_values.shape[0]
    adj3 = adjoint.reshape(layers, cy, cx)
    traj3 = trajectory.reshape(layers, cy, cx)

    def edges(depth):
        top = pl.BlockSpec((depth, 8, cx), lambda i: (0, cy // 8 - 1, 0))
        bot = pl.BlockSpec((depth, 8, cx), lambda i: (0, 0, 0))
        west = pl.BlockSpec((depth, cy, LANES), lambda i: (0, 0, 0))
        east = pl.BlockSpec((depth, cy, LANES), lambda i: (0, 0, cx // LANES - 1))
        return [top, bot, west, east]

    def whole(shape):
        return pl.BlockSpec(shape, lambda i: (0,) * len(shape))

    def f32(*shape):
        return jax.ShapeDtypeStruct(shape, F32)

    packed = -(-(layers + levels) // 8) * 8
    row_shape, col_shape, obs_shape = (NSUB, packed, cx), (cy, 2 * LANES), (n, 2 * CAP, LANES)
    shapes = [row_shape, row_shape, col_shape, col_shape, obs_shape]
    packs = pl.pallas_call(
        functools.partial(pack_kernel, n, levels),
        grid=(1,),
        out_shape=[f32(*s) for s in shapes],
        in_specs=edges(layers) + edges(levels) + edges(levels)
        + [whole((1, rows))] * 3 + [whole((rows, LANES))],
        out_specs=[whole(s) for s in shapes],
        compiler_params=pltpu.CompilerParams(vmem_limit_bytes=60 << 20),
        name="pack",
    )(
        *[adj3] * 4, *[land_mask] * 4, *[diffusivity] * 4,
        obs_owner.reshape(1, rows), obs_weight.reshape(1, rows), obs_offset.reshape(1, rows),
        obs_values,
    )

    corner = (8, 2 * LANES)
    came = [row_shape, row_shape, col_shape, col_shape, corner, corner, corner, corner]
    fold_shape = (n_lon,) + row_shape
    *halos, fold, got = pl.pallas_call(
        functools.partial(exchange_kernel, n_lon, n_lat),
        out_shape=[f32(*s) for s in came + [fold_shape, obs_shape]],
        in_specs=[pl.BlockSpec(memory_space=pl.ANY)] * 5,
        out_specs=[pl.BlockSpec(memory_space=pl.ANY)] * 10,
        scratch_shapes=[
            pltpu.SemaphoreType.DMA((8,)), pltpu.SemaphoreType.DMA((8,)),
            pltpu.SemaphoreType.DMA((n_lon,)), pltpu.SemaphoreType.DMA((n_lon,)),
            pltpu.SemaphoreType.DMA((n,)), pltpu.SemaphoreType.DMA((n,)),
            pltpu.SemaphoreType.DMA((2,)),
        ],
        compiler_params=pltpu.CompilerParams(collective_id=0, has_side_effects=True),
        name="exchange",
    )(*packs)

    meta = got[:, CAP:, :2].reshape(n * CAP * 2)
    smem = pl.BlockSpec(memory_space=pltpu.SMEM)
    level3 = pl.BlockSpec((1, cy, cx), lambda i: (i, 0, 0))
    level4 = pl.BlockSpec((fields, 1, cy, cx), lambda i: (0, i, 0, 0))
    return pl.pallas_call(
        functools.partial(main_kernel, n, n_lon, n_lat, layers),
        grid=(levels,),
        out_shape=f32(*adjoint.shape),
        in_specs=[smem, smem, level4, level3, level3, whole((1, cy)),
                  whole((layers, cy, cx)), whole(obs_shape)]
        + [whole(s) for s in came] + [whole(fold_shape)],
        out_specs=level4,
        scratch_shapes=[
            VMEM((layers, cy, cx), F32),
            VMEM((NSUB, packed, cx + LANES), F32),
            VMEM((cy + 8, cx + LANES), F32),
        ],
        compiler_params=pltpu.CompilerParams(vmem_limit_bytes=56 << 20),
        name="mix",
    )(
        meta, fold_partner, adjoint, diffusivity, land_mask,
        coriolis.reshape(1, cy), traj3, got, *halos, fold,
    )


def solution(mesh):
    return jax.shard_map(
        functools.partial(per_device, mesh.shape["lon"], mesh.shape["lat"]),
        mesh=mesh,
        in_specs=(
            P(None, None, "lat", "lon"),
            P(None, None, "lat", "lon"),
            P(None, "lat", "lon"),
            P(None, "lat", "lon"),
            P("lat"),
            P(("lon", "lat"), None),
            P(("lon", "lat")),
            P(("lon", "lat"), None),
            P(("lon", "lat")),
            P("lon"),
        ),
        out_specs=P(None, None, "lat", "lon"),
        check_vma=False,
    )
```

```python
import functools

import jax
import jax.numpy as jnp
from jax import lax
from jax.experimental import pallas as pl
from jax.experimental.pallas import tpu as pltpu
from jax.sharding import PartitionSpec as P

NSUB = 3
CAP = 8
LANES = 128
MESH = pl.DeviceIdType.MESH
VMEM = pltpu.VMEM
F32 = jnp.float32


def dot(left, right, dims, precision=lax.Precision.HIGHEST):
    return lax.dot_general(
        left, right, (dims, ((), ())), precision=precision, preferred_element_type=F32
    )


def pack_kernel(
    n, levels,
    adj_top, adj_bot, adj_w, adj_e, wet_top, wet_bot, wet_w, wet_e,
    dif_top, dif_bot, dif_w, dif_e, owner, weight, offset, values,
    row_top, row_bot, col_w, col_e, obs,
):
    layers = adj_top.shape[0]
    for out in (row_top, row_bot):
        out[...] = jnp.zeros_like(out)

    def state_level(layer, carry):
        k = lax.rem(layer, levels)
        top = adj_top[layer] * wet_top[k].astype(F32)
        bot = adj_bot[layer] * wet_bot[k].astype(F32)
        for r in range(NSUB):
            row_top[r, pl.ds(layer, 1), :] = top[8 - NSUB + r : 8 - NSUB + r + 1]
            row_bot[r, pl.ds(layer, 1), :] = bot[r : r + 1]
        return columns(
            layer, adj_w[layer] * wet_w[k].astype(F32), adj_e[layer] * wet_e[k].astype(F32), carry
        )

    def columns(place, west, east, carry):
        lane = lax.broadcasted_iota(jnp.int32, west.shape, 1)
        first = NSUB * place
        here = (lane >= first) & (lane < first + NSUB)
        west = pltpu.roll(west, first, 1)
        east = pltpu.roll(east, lax.rem(first + NSUB, LANES), 1)
        return jnp.where(here, west, carry[0]), jnp.where(here, east, carry[1])

    def dif_level(k, carry):
        top, bot = dif_top[k], dif_bot[k]
        for r in range(NSUB):
            row_top[r, pl.ds(layers + k, 1), :] = top[8 - NSUB + r : 8 - NSUB + r + 1]
            row_bot[r, pl.ds(layers + k, 1), :] = bot[r : r + 1]
        return columns(k, dif_w[k], dif_e[k], carry)

    zero = jnp.zeros(adj_w.shape[1:], F32)
    west, east = lax.fori_loop(0, layers, state_level, (zero, zero))
    col_w[:, :LANES], col_e[:, :LANES] = west, east
    west, east = lax.fori_loop(0, levels, dif_level, (zero, zero))
    col_w[:, LANES:], col_e[:, LANES:] = west, east

    rows = values.shape[0]
    own = owner[...]
    one_hot = (lax.broadcasted_iota(jnp.int32, (n, rows), 0) == own).astype(F32)
    earlier_than = (
        lax.broadcasted_iota(jnp.int32, (rows, rows), 0)
        < lax.broadcasted_iota(jnp.int32, (rows, rows), 1)
    ).astype(F32)
    earlier = dot(one_hot, earlier_than, ((1,), (0,)), lax.Precision.DEFAULT)
    slot = jnp.sum(earlier * one_hot, axis=0, keepdims=True).astype(jnp.int32)
    dest = own * CAP + slot
    hit = lax.broadcasted_iota(jnp.int32, (n * CAP, rows), 0) == dest
    sent = dot(hit.astype(F32), values[...], ((1,), (0,)))
    w = jnp.sum(jnp.where(hit, weight[...], 0.0), axis=1, keepdims=True)
    o = jnp.sum(jnp.where(hit, offset[...].astype(F32), 0.0), axis=1, keepdims=True)
    lane = lax.broadcasted_iota(jnp.int32, (n * CAP, LANES), 1)
    meta = jnp.where(lane == 0, w, o)
    obs[:, :CAP, :] = sent.reshape(n, CAP, LANES)
    obs[:, CAP:, :] = meta.reshape(n, CAP, LANES)


def exchange_kernel(
    n_lon, n_lat,
    row_top, row_bot, col_w, col_e, obs,
    north, south, west, east, corner_nw, corner_ne, corner_sw, corner_se, fold, got,
    send_sem, recv_sem, fold_send, fold_recv, obs_send, obs_recv, local_sem,
):
    n = n_lon * n_lat
    lon, lat = lax.axis_index("lon"), lax.axis_index("lat")
    me = lon * n_lat + lat
    right, left = lax.rem(lon + 1, n_lon), lax.rem(lon + n_lon - 1, n_lon)
    low, high = lat == 0, lat == n_lat - 1
    up, down = lax.rem(lat + 1, n_lat), lax.rem(lat + n_lat - 1, n_lat)

    barrier = pltpu.get_barrier_semaphore()

    @pl.loop(1, n)
    def _(step):
        peer = lax.rem(me + step, n)
        pl.semaphore_signal(
            barrier, inc=1, device_id=(peer // n_lat, lax.rem(peer, n_lat)), device_id_type=MESH
        )

    pl.semaphore_wait(barrier, n - 1)

    def remote(src, dst, sems, rsems, i, target):
        return pltpu.make_async_remote_copy(
            src_ref=src, dst_ref=dst, send_sem=sems.at[i], recv_sem=rsems.at[i],
            device_id=target, device_id_type=MESH,
        )

    halo = functools.partial(
        lambda i, src, dst, target: remote(src, dst, send_sem, recv_sem, i, target)
    )
    last = col_w.shape[0] - 8
    lifted = [
        halo(0, row_top, south, (lon, up)),
        halo(1, col_e.at[pl.ds(last, 8)], corner_sw, (right, up)),
        halo(2, col_w.at[pl.ds(last, 8)], corner_se, (left, up)),
    ]
    lowered = [
        halo(3, row_bot, north, (lon, down)),
        halo(4, col_e.at[pl.ds(0, 8)], corner_nw, (right, down)),
        halo(5, col_w.at[pl.ds(0, 8)], corner_ne, (left, down)),
    ]
    level = [halo(6, col_e, west, (right, lat)), halo(7, col_w, east, (left, lat))]

    def fold_copy(step, slot):
        peer = lax.rem(lon + step, n_lon)
        return remote(row_top, fold.at[slot], fold_send, fold_recv, step, (peer, lat))

    def obs_copy(step, slot):
        peer = lax.rem(me + step, n)
        return remote(
            obs.at[peer], got.at[slot], obs_send, obs_recv, step,
            (peer // n_lat, lax.rem(peer, n_lat)),
        )

    own_fold = pltpu.make_async_copy(row_top, fold.at[lon], local_sem.at[0])
    own_obs = pltpu.make_async_copy(obs.at[me], got.at[me], local_sem.at[1])

    @pl.when(high)
    def _():
        for step in range(1, n_lon):
            fold_copy(step, lon).start()
        own_fold.start()

    @pl.when(jnp.logical_not(high))
    def _():
        for copy in lifted:
            copy.start()

    @pl.when(jnp.logical_not(low))
    def _():
        for copy in lowered:
            copy.start()

    for copy in level:
        copy.start()

    @pl.loop(1, n)
    def _(step):
        obs_copy(step, me).start()

    own_obs.start()

    @pl.when(high)
    def _():
        for step in range(1, n_lon):
            fold_copy(step, lax.rem(lon + n_lon - step, n_lon)).wait_recv()
            fold_copy(step, lon).wait_send()
        own_fold.wait()

    @pl.when(jnp.logical_not(high))
    def _():
        for copy in lifted:
            copy.wait_send()
        for copy in lowered:
            copy.wait_recv()

    @pl.when(jnp.logical_not(low))
    def _():
        for copy in lowered:
            copy.wait_send()
        for copy in lifted:
            copy.wait_recv()

    for copy in level:
        copy.wait()

    @pl.loop(1, n)
    def _(step):
        obs_copy(step, lax.rem(me + n - step, n)).wait_recv()
        obs_copy(step, me).wait_send()

    own_obs.wait()


def main_kernel(
    n, n_lon, n_lat, layers,
    meta, partner,
    adj, dif, wet_ref, coriolis, traj, got,
    north, south, west, east, corner_nw, corner_ne, corner_sw, corner_se, fold,
    out, forcing, rim, ext,
):
    k = pl.program_id(0)
    fields, _, cy, cx = adj.shape
    levels = layers // fields
    lat = lax.axis_index("lat")
    low, high = lat == 0, lat == n_lat - 1
    wide = cx + LANES
    segs = cx // LANES
    sub8 = lax.broadcasted_iota(jnp.int32, (8, LANES), 0)

    @pl.when(k == 0)
    def _():
        forcing[...] = jnp.zeros_like(forcing)
        ext[...] = jnp.zeros_like(ext)

        @pl.loop(0, n)
        def _(block):
            for s in range(CAP):
                place = meta[(block * CAP + s) * 2 + 1].astype(jnp.int32)
                lanes = pl.ds(pl.multiple_of(lax.rem(place, segs) * LANES, LANES), LANES)
                rest = place // segs
                y, layer = lax.rem(rest, cy), rest // cy
                tile = pl.ds(pl.multiple_of(y // 8 * 8, 8), 8)
                misfit = meta[(block * CAP + s) * 2] * (
                    traj[layer, tile, lanes] - got[block, s : s + 1, :]
                )
                forcing[layer, tile, lanes] = forcing[layer, tile, lanes] + jnp.where(
                    sub8 == lax.rem(y, 8), misfit, 0.0
                )

        @pl.when(jnp.logical_not(high))
        def _():
            rim[:, :, :cx] = north[...]

        @pl.when(high)
        def _():
            nx = n_lon * cx
            lane = lax.broadcasted_iota(jnp.int32, (cx, wide), 1)
            lane = jnp.where(lane < cx + LANES // 2, lane, lane - wide)
            column = partner[0] - lane
            column = jnp.where(column < 0, column + nx, column)
            column = jnp.where(column >= nx, column - nx, column)
            within = lax.broadcasted_iota(jnp.int32, (cx, wide), 0)
            deep = fold.shape[2]
            total = jnp.zeros((NSUB * deep, wide), F32)
            for t in range(n_lon):
                pick = (within + t * cx == column).astype(F32).astype(jnp.bfloat16)
                left = fold[t].reshape(NSUB * deep, cx)
                for part in range(3):
                    piece = left.astype(jnp.bfloat16)
                    left = left - piece.astype(F32)
                    total = total + dot(piece, pick, ((1,), (0,)), None)
            for r in range(NSUB):
                rim[r] = total[(NSUB - 1 - r) * deep : (NSUB - r) * deep]

    lane = lax.broadcasted_iota(jnp.int32, (cy, LANES), 1)
    lane8 = lax.broadcasted_iota(jnp.int32, (8, LANES), 1)

    def surround(place, row, side, sign):
        cols = pl.ds(side * LANES, LANES)
        shift_e = lax.rem(LANES - NSUB * place, LANES)
        shift_w = lax.rem(2 * LANES - NSUB - NSUB * place, LANES)
        ext[:cy, cx:] = jnp.where(
            lane < LANES // 2,
            pltpu.roll(east[:, cols], shift_e, 1),
            pltpu.roll(west[:, cols], shift_w, 1),
        )

        def corner(e_ref, w_ref, absent):
            both = jnp.where(
                lane8 < LANES // 2,
                pltpu.roll(e_ref[:, cols], shift_e, 1),
                pltpu.roll(w_ref[:, cols], shift_w, 1),
            )
            return jnp.where(absent, 0.0, both)

        ext[cy:, cx:] = jnp.where(
            sub8 < 4,
            corner(corner_ne, corner_nw, high),
            corner(corner_se, corner_sw, low),
        )
        for r in range(NSUB):
            ext[cy + r : cy + r + 1, :cx] = sign * rim[r, pl.ds(row, 1), :][:, :cx]
            line = south[r, pl.ds(row, 1), :]
            at = cy + 8 - NSUB + r
            ext[at : at + 1, :cx] = jnp.where(low, 0.0, line)

        @pl.when(high)
        def _():
            for r in range(NSUB):
                ext[cy + r : cy + r + 1, cx:] = sign * rim[r, pl.ds(row, 1), :][:, cx:]

    ext[:cy, :cx] = dif[0]
    surround(k, layers + k, 1, 1.0)
    coeffs = ext[...]
    wet = wet_ref[0].astype(F32)
    mixed = []
    for f in range(fields):
        ext[:cy, :cx] = adj[f, 0] * wet
        layer = f * levels + k
        surround(layer, layer, 0, jnp.where(high, 1.0 if f < 2 else -1.0, 1.0))
        work = ext[...]
        for _ in range(NSUB):
            near = (
                pltpu.roll(work, wide - 1, 1)
                + pltpu.roll(work, 1, 1)
                + pltpu.roll(work, cy + 7, 0)
                + pltpu.roll(work, 1, 0)
            )
            work = work + coeffs * (near - 4.0 * work)
        mixed.append(work[:cy, :cx])
    line = coriolis[...]
    square = lax.broadcasted_iota(jnp.int32, (cy, cy), 0) == lax.broadcasted_iota(
        jnp.int32, (cy, cy), 1
    )
    turn = jnp.sum(jnp.where(square, line, 0.0), axis=1, keepdims=True)
    u, v = mixed[2] - turn * mixed[3], mixed[3] + turn * mixed[2]
    for f, m in enumerate((mixed[0], mixed[1], u, v)):
        out[f, 0] = wet * (m + forcing[f * levels + k])


def per_device(
    n_lon, n_lat,
    adjoint, trajectory, diffusivity, land_mask, coriolis,
    obs_values, obs_weight, obs_owner, obs_offset, fold_partner,
):
    n = n_lon * n_lat
    fields, levels, cy, cx = adjoint.shape
    layers = fields * levels
    rows = obs_values.shape[0]
    adj3 = adjoint.reshape(layers, cy, cx)
    traj3 = trajectory.reshape(layers, cy, cx)

    def edges(depth):
        top = pl.BlockSpec((depth, 8, cx), lambda i: (0, cy // 8 - 1, 0))
        bot = pl.BlockSpec((depth, 8, cx), lambda i: (0, 0, 0))
        west = pl.BlockSpec((depth, cy, LANES), lambda i: (0, 0, 0))
        east = pl.BlockSpec((depth, cy, LANES), lambda i: (0, 0, cx // LANES - 1))
        return [top, bot, west, east]

    def whole(shape):
        return pl.BlockSpec(shape, lambda i: (0,) * len(shape))

    def f32(*shape):
        return jax.ShapeDtypeStruct(shape, F32)

    packed = -(-(layers + levels) // 8) * 8
    row_shape, col_shape, obs_shape = (NSUB, packed, cx), (cy, 2 * LANES), (n, 2 * CAP, LANES)
    shapes = [row_shape, row_shape, col_shape, col_shape, obs_shape]
    packs = pl.pallas_call(
        functools.partial(pack_kernel, n, levels),
        grid=(1,),
        out_shape=[f32(*s) for s in shapes],
        in_specs=edges(layers) + edges(levels) + edges(levels)
        + [whole((1, rows))] * 3 + [whole((rows, LANES))],
        out_specs=[whole(s) for s in shapes],
        compiler_params=pltpu.CompilerParams(vmem_limit_bytes=60 << 20),
        name="pack",
    )(
        *[adj3] * 4, *[land_mask] * 4, *[diffusivity] * 4,
        obs_owner.reshape(1, rows), obs_weight.reshape(1, rows), obs_offset.reshape(1, rows),
        obs_values,
    )

    corner = (8, 2 * LANES)
    came = [row_shape, row_shape, col_shape, col_shape, corner, corner, corner, corner]
    fold_shape = (n_lon,) + row_shape
    *halos, fold, got = pl.pallas_call(
        functools.partial(exchange_kernel, n_lon, n_lat),
        out_shape=[f32(*s) for s in came + [fold_shape, obs_shape]],
        in_specs=[pl.BlockSpec(memory_space=pl.ANY)] * 5,
        out_specs=[pl.BlockSpec(memory_space=pl.ANY)] * 10,
        scratch_shapes=[
            pltpu.SemaphoreType.DMA((8,)), pltpu.SemaphoreType.DMA((8,)),
            pltpu.SemaphoreType.DMA((n_lon,)), pltpu.SemaphoreType.DMA((n_lon,)),
            pltpu.SemaphoreType.DMA((n,)), pltpu.SemaphoreType.DMA((n,)),
            pltpu.SemaphoreType.DMA((2,)),
        ],
        compiler_params=pltpu.CompilerParams(collective_id=0, has_side_effects=True),
        name="exchange",
    )(*packs)

    meta = got[:, CAP:, :2].reshape(n * CAP * 2)
    smem = pl.BlockSpec(memory_space=pltpu.SMEM)
    level3 = pl.BlockSpec((1, cy, cx), lambda i: (i, 0, 0))
    level4 = pl.BlockSpec((fields, 1, cy, cx), lambda i: (0, i, 0, 0))
    return pl.pallas_call(
        functools.partial(main_kernel, n, n_lon, n_lat, layers),
        grid=(levels,),
        out_shape=f32(*adjoint.shape),
        in_specs=[smem, smem, level4, level3, level3, whole((1, cy)),
                  whole((layers, cy, cx)), whole(obs_shape)]
        + [whole(s) for s in came] + [whole(fold_shape)],
        out_specs=level4,
        scratch_shapes=[
            VMEM((layers, cy, cx), F32),
            VMEM((NSUB, packed, cx + LANES), F32),
            VMEM((cy + 8, cx + LANES), F32),
        ],
        compiler_params=pltpu.CompilerParams(vmem_limit_bytes=56 << 20),
        name="mix",
    )(
        meta, fold_partner, adjoint, diffusivity, land_mask,
        coriolis.reshape(1, cy), traj3, got, *halos, fold,
    )


def solution(mesh):
    return jax.shard_map(
        functools.partial(per_device, mesh.shape["lon"], mesh.shape["lat"]),
        mesh=mesh,
        in_specs=(
            P(None, None, "lat", "lon"),
            P(None, None, "lat", "lon"),
            P(None, "lat", "lon"),
            P(None, "lat", "lon"),
            P("lat"),
            P(("lon", "lat"), None),
            P(("lon", "lat")),
            P(("lon", "lat"), None),
            P(("lon", "lat")),
            P("lon"),
        ),
        out_specs=P(None, None, "lat", "lon"),
        check_vma=False,
    )
```
